32 devices in a mesh: trace: 4 (over x, core), seq: 8 (over z, y).
Axes of the slice: x: 2, y: 2, z: 4, core: 2. Of those that a mesh axis runs over, the one named last changes fastest.
Arguments:
- tokens: bfloat16 [32768, 1024], P(('trace', 'seq')), parts along dimension 0, may hold values from -6 to 6
- norm_gain: float32 [1024], replicated, may hold values from 0.1 to 1.9
- w_qkv: bfloat16 [1024, 3072], replicated, may hold values from -0.02734375 to 0.02734375
- conv_weight: float32 [4, 3072], replicated, may hold values from -3 to 3
- head_gain: float32 [1024], replicated, may hold values from 0.1 to 1.9
- w_out: bfloat16 [1024, 1024], replicated, may hold values from -0.1875 to 0.1875
Outputs:
- layer_out: bfloat16 [32768, 1024], P(('trace', 'seq')), parts along dimension 0
The draws below stay inside these ranges and needn't reach their ends.
There are 4 independent parts, one for each index of `trace`. The reference program is written for one: setup_inputs(seed, part) draws one part's arguments, and reference() takes and returns one part's arrays. A program takes and returns all parts, laid end to end along the dimension named above; an argument that names none is the same for every part. Nothing has to cross between parts.
All inputs are finite; a program needn't handle non-finite values.
Results may differ from the reference program's by a relative error of at most 0.012.
Values may be sent and summed in bfloat16 or wider, within the bound.
A program may use at most 128 MiB of HBM per device.

```python
import jax
import jax.numpy as jnp
from jax import lax

H = 8
DH = 128
D = 1024
KW = 4
TOK_DEV = 1024
TOKENS = 8192


def level_of(own_key, dims, pieces, least, high):
    gain, own = 1.0, jax.random.fold_in(own_key, 6)
    for position, shards_of in pieces:
        draws = jnp.exp(jax.random.uniform(jax.random.fold_in(own, position), (shards_of,), jnp.float32, least / len(pieces), high / len(pieces)))
        gain = gain * jnp.repeat(draws, dims[position] // shards_of).reshape([-1 if axis == position else 1 for axis in range(len(dims))])
    return gain


def normal_values(rng, shape, deviation, limit, shards=(), held_as=jnp.bfloat16):
    result = jax.random.normal(rng, shape, jnp.float32) * deviation
    if len(shards) > 0:
        result = level_of(rng, shape, shards, -0.22, 0.18) * result
    return jnp.clip(result, min=-limit, max=limit).astype(held_as)


def setup_inputs(seed: int = 0, part: int = 0) -> dict:
    keys = jax.random.split(jax.random.key(seed), 7)
    part_splits = jax.random.split(jax.random.fold_in(keys[6], part), 7)
    tokens = normal_values(part_splits[0], (TOKENS, D), 1.0, 6.0, ((0, 8),))
    norm_gain = jnp.clip(1.0 + 0.18 * jax.random.normal(keys[1], (D,), jnp.float32), 0.1, 1.9)
    w_qkv = normal_values(keys[2], (D, 3 * D), (44 * D) ** -0.5, 0.02734375)
    conv_weight = normal_values(keys[3], (KW, 3 * D), 0.6, 3.0, (), jnp.float32)
    head_gain = jnp.clip(1.0 + 0.18 * jax.random.normal(keys[4], (D,), jnp.float32), 0.1, 1.9)
    w_out = normal_values(keys[5], (D, D), D ** -0.5, 0.1875)
    return dict(tokens=tokens, norm_gain=norm_gain, w_qkv=w_qkv, conv_weight=conv_weight, head_gain=head_gain, w_out=w_out)


def conv_silu(projected, conv_weight):
    length = projected.shape[0]
    padded = jnp.concatenate([jnp.zeros((KW - 1, projected.shape[1]), jnp.bfloat16), projected], 0)
    summed = jnp.zeros(projected.shape, jnp.float32)
    for offset in range(KW):
        begin = KW - 1 - offset
        summed = summed + conv_weight[offset].astype(jnp.float32) * padded[begin:begin + length].astype(jnp.float32)
    return jax.nn.silu(summed).astype(jnp.bfloat16)

def reference(tokens, norm_gain, w_qkv, conv_weight, head_gain, w_out):
    highest = lax.Precision.HIGHEST
    tokens_f = tokens.astype(jnp.float32)
    normed = (tokens_f * lax.rsqrt(lax.optimization_barrier(jnp.mean(tokens_f * tokens_f, -1, keepdims=True)) + 1e-06) * norm_gain.astype(jnp.float32)).astype(jnp.bfloat16)
    projected = jnp.dot(normed, w_qkv, preferred_element_type=jnp.float32).astype(jnp.bfloat16)
    mixed = conv_silu(projected, conv_weight)
    length = mixed.shape[0]
    block_rows = min(512, TOK_DEV)
    count = length // block_rows
    query_rows = mixed[:, :D].reshape(count, block_rows, H, DH)
    key_rows = mixed[:, D:2 * D].reshape(count, block_rows, H, DH)
    value_rows = mixed[:, 2 * D:].reshape(count, block_rows, H, DH)
    causal = jnp.tril(jnp.ones((block_rows, block_rows), jnp.bool_))

    def advance(carried, blocks):
        query_f = blocks[0].astype(jnp.float32)
        key_f = blocks[1].astype(jnp.float32)
        value_f = blocks[2].astype(jnp.float32)
        carried_part = jnp.einsum('thd,hde->the', query_f, carried, precision=highest)
        scores = jnp.einsum('thd,shd->hts', query_f, key_f, precision=highest)
        scores = jnp.where(causal[None], scores, 0.0).astype(jnp.bfloat16)
        local_part = jnp.einsum('hts,she->the', scores.astype(jnp.float32), value_f, precision=highest)
        carried = carried + jnp.einsum('thd,the->hde', key_f, value_f, precision=highest)
        return (carried, carried_part + local_part)
    _, attended = lax.scan(advance, jnp.zeros((H, DH, DH), jnp.float32), (query_rows, key_rows, value_rows))
    attended = attended.reshape(length, H, DH)
    scaled = attended * lax.rsqrt(lax.optimization_barrier(jnp.mean(attended * attended, -1, keepdims=True)) + 1e-05)
    headed = (scaled.reshape(length, D) * head_gain.astype(jnp.float32)).astype(jnp.bfloat16)
    return jnp.dot(headed, w_out, preferred_element_type=jnp.float32).astype(jnp.bfloat16)
```

```python
import functools

import jax
import jax.numpy as jnp
from jax import lax
from jax.experimental import pallas as pl
from jax.experimental.pallas import tpu as pltpu
from jax.sharding import PartitionSpec as P

H = 8
DH = 128
KW = 4
PW = 2 * DH
PAIRS = H // 2
HALO = 16
BLK = 256
SUB = 64
SKEW = 2

bf16 = jnp.bfloat16
f32 = jnp.float32


def kernel(
    n_seq, rows,
    tok_hbm, ng_hbm, w_hbm, cw_hbm, hg_hbm, wo_hbm, out_hbm,
    tok, halo, xn, ng, cw, hg, w, wo, pf, qs, ks, vs, att, hd, ost, cst, bd,
    ysend, yrecv, zsend, zrecv,
    tok_sem, w_sem, small_sem, wo_sem, out_sem,
    halo_ssem, halo_rsem, y_ssem, y_rsem, z_ssem, z_rsem,
):
    d_model = tok.shape[1]
    nblk = rows // BLK
    me = lax.axis_index("seq")
    odd = lax.rem(me, 2)
    place = me // 2
    depth = n_seq // 2
    partner = me + 1 - 2 * odd

    tok_rows = rows // 4
    def tok_copy(i):
        r = pl.ds(i * tok_rows, tok_rows)
        return pltpu.make_async_copy(tok_hbm.at[r], tok.at[r], tok_sem.at[i])
    def w_copy(c):
        return pltpu.make_async_copy(w_hbm.at[:, pl.ds(pl.multiple_of(c * PW, PW), PW)], w.at[c], w_sem.at[c])
    def wo_copy(c):
        return pltpu.make_async_copy(wo_hbm.at[:, pl.ds(pl.multiple_of(c * PW, PW), PW)], wo.at[c], wo_sem.at[c])
    def small_copies():
        return [
            pltpu.make_async_copy(ng_hbm, ng, small_sem.at[0]),
            pltpu.make_async_copy(cw_hbm, cw, small_sem.at[1]),
            pltpu.make_async_copy(hg_hbm, hg, small_sem.at[2]),
        ]

    barrier = pltpu.get_barrier_semaphore()
    for delta in (-2, -1, 1, 2):
        other = me + delta
        @pl.when((other >= 0) & (other < n_seq))
        def _():
            pl.semaphore_signal(
                barrier, inc=1, device_id={"seq": other}, device_id_type=pl.DeviceIdType.MESH
            )
    for c in small_copies():
        c.start()
    for i in range(4):
        tok_copy(i).start()
    for g in range(PAIRS):
        w_copy(PAIRS + g).start()
        w_copy(2 * PAIRS + g).start()
    for g in range(PAIRS):
        w_copy(g).start()
    for g in range(PAIRS):
        wo_copy(g).start()
    before = jnp.minimum(me, 2)
    after = jnp.minimum(n_seq - 1 - me, 2)
    pl.semaphore_wait(barrier, before + after)

    halo_copy = pltpu.make_async_remote_copy(
        src_ref=tok_hbm.at[pl.ds(rows - HALO, HALO)],
        dst_ref=halo,
        send_sem=halo_ssem,
        recv_sem=halo_rsem,
        device_id={"seq": me + 1},
        device_id_type=pl.DeviceIdType.MESH,
    )
    @pl.when(me < n_seq - 1)
    def _():
        halo_copy.start()
    @pl.when(me == 0)
    def _():
        halo[...] = jnp.zeros(halo.shape, bf16)
    @pl.when(place == 0)
    def _():
        zrecv[...] = jnp.zeros(zrecv.shape, bf16)
    bd[...] = jnp.zeros(bd.shape, bf16)

    def y_copy(g):
        return pltpu.make_async_remote_copy(
            src_ref=ysend.at[g], dst_ref=yrecv.at[g], send_sem=y_ssem.at[g], recv_sem=y_rsem.at[g],
            device_id={"seq": partner}, device_id_type=pl.DeviceIdType.MESH,
        )

    def z_copy(g):
        return pltpu.make_async_remote_copy(
            src_ref=zsend.at[g], dst_ref=zrecv.at[g], send_sem=z_ssem.at[g], recv_sem=z_rsem.at[g],
            device_id={"seq": me + 2}, device_id_type=pl.DeviceIdType.MESH,
        )

    def slot(p):
        g = p - SKEW * place

        @pl.when((g >= 0) & (g < PAIRS) & (place < depth - 1))
        def _():
            y_copy(g).wait_recv()

            @pl.when(place > 0)
            def _():
                z_copy(g).wait_recv()

            zsend[g] = (
                ysend[g].astype(f32) + yrecv[g].astype(f32) + zrecv[g].astype(f32)
            ).astype(bf16)
            z_copy(g).start()

    def norm(x, gain):
        xf = x.astype(f32)
        scale = lax.rsqrt(jnp.mean(xf * xf, -1, keepdims=True) + 1e-06)
        return (xf * scale * gain).astype(bf16)

    for c in small_copies():
        c.wait()
    step = 32
    for i in range(4):
        tok_copy(i).wait()

        @pl.loop(0, tok_rows // step)
        def _(t):
            at = pl.multiple_of(i * tok_rows + t * step, step)
            xn[pl.ds(pl.multiple_of(HALO + at, 16), step), :] = norm(tok[pl.ds(at, step), :], ng[...])
    @pl.when(me > 0)
    def _():
        halo_copy.wait_recv()
    xn[0:HALO, :] = norm(halo[...], ng[...])

    half = rows // 2

    def project(c, slot_pf, dst, g):
        taps = [
            [0.5 * cw[j : j + 1, pl.ds(pl.multiple_of(c * PW + h * DH, DH), DH)] for j in range(KW)]
            for h in range(2)
        ]
        for part in range(2):
            lo = 0 if part == 0 else HALO + half
            hi = HALO + half * (part + 1)
            p = jnp.dot(xn[lo:hi, :], w[c], preferred_element_type=f32)
            for h in range(2):
                pf[slot_pf, h, lo:hi, :] = p[:, h * DH : (h + 1) * DH]
            for h in range(2):
                for r in range(part * half, (part + 1) * half, SUB):
                    acc = taps[h][0] * pf[slot_pf, h, HALO + r : HALO + r + SUB, :]
                    for j in range(1, KW):
                        acc += taps[h][j] * pf[slot_pf, h, HALO + r - j : HALO + r - j + SUB, :]
                    dst[g, r : r + SUB, h * DH : (h + 1) * DH] = (acc + acc * jnp.tanh(acc)).astype(bf16)

    @pl.loop(0, PAIRS)
    def _(g):
        w_copy(PAIRS + g).wait()
        w_copy(2 * PAIRS + g).wait()
        project(PAIRS + g, 0, ks, g)
        project(2 * PAIRS + g, 1, vs, g)
        total = None
        for b in range(nblk):
            r = slice(b * BLK, (b + 1) * BLK)
            s = lax.dot_general(
                ks[g, r, :], vs[g, r, :], (((0,), (0,)), ((), ())), preferred_element_type=f32
            )
            s = [s[0:DH, 0:DH], s[DH:PW, DH:PW]]
            total = s if total is None else [total[0] + s[0], total[1] + s[1]]
            if b < nblk - 1:
                cst[g, b, 0] = total[0]
                cst[g, b, 1] = total[1]
        ysend[g, 0] = total[0].astype(bf16)
        ysend[g, 1] = total[1].astype(bf16)
        y_copy(g).start()
        slot(g - 1)

    causal = (
        lax.broadcasted_iota(jnp.int32, (BLK, BLK), 0)
        >= lax.broadcasted_iota(jnp.int32, (BLK, BLK), 1)
    )

    @pl.loop(0, PAIRS)
    def _(g):
        w_copy(g).wait()
        project(g, 0, qs, g)
        for h in range(2):
            c = slice(h * DH, (h + 1) * DH)
            for b in range(nblk):
                r = slice(b * BLK, (b + 1) * BLK)
                s = lax.dot_general(
                    qs[g, r, c], ks[g, r, c], (((1,), (1,)), ((), ())), preferred_element_type=f32
                )
                s = jnp.where(causal, s, 0.0).astype(bf16)
                att[g, r, c] = jnp.dot(s, vs[g, r, c], preferred_element_type=f32)
        slot(PAIRS - 1 + g)

    first_left = 2 * PAIRS - 1
    for p in range(first_left, PAIRS + SKEW * max(depth - 2, 0)):
        slot(p)

    oddf = odd.astype(f32)

    @pl.loop(0, PAIRS)
    def _(g):
        @pl.when(place == depth - 1)
        def _():
            y_copy(g).wait_recv()

            @pl.when(place > 0)
            def _():
                z_copy(g).wait_recv()

        cols = pl.multiple_of(g * PW, PW)
        for h in range(2):
            c = slice(h * DH, (h + 1) * DH)
            prefix = zrecv[g, h].astype(f32) + oddf * yrecv[g, h].astype(f32)
            for b in range(nblk):
                carried = prefix if b == 0 else prefix + cst[g, b - 1, h]
                bd[b, c, c] = carried.astype(bf16)
        for b in range(nblk):
            r = slice(b * BLK, (b + 1) * BLK)
            both = att[g, r, :] + jnp.dot(qs[g, r, :], bd[b], preferred_element_type=f32)
            for h in range(2):
                a = both[:, h * DH : (h + 1) * DH]
                at = pl.multiple_of(g * PW + h * DH, DH)
                scale = lax.rsqrt(jnp.mean(a * a, -1, keepdims=True) + 1e-05)
                hd[r, pl.ds(at, DH)] = (a * scale * hg[:, pl.ds(at, DH)]).astype(bf16)

    def out_copy(c):
        return pltpu.make_async_copy(
            ost.at[c], out_hbm.at[:, pl.ds(pl.multiple_of(c * PW, PW), PW)], out_sem.at[c]
        )

    @pl.loop(0, d_model // PW)
    def _(c):
        wo_copy(c).wait()
        ost[c] = jnp.dot(hd[...], wo[c], preferred_element_type=f32).astype(bf16)
        out_copy(c).start()

    @pl.when(me < n_seq - 1)
    def _():
        halo_copy.wait_send()
    for g in range(PAIRS):
        y_copy(g).wait_send()

        @pl.when(place < depth - 1)
        def _():
            z_copy(g).wait_send()
    for c in range(d_model // PW):
        out_copy(c).wait()


def local(n_seq, tokens, norm_gain, w_qkv, conv_weight, head_gain, w_out):
    rows, d_model = tokens.shape
    nblk = rows // BLK
    groups = 3 * PAIRS
    any_spec = pl.BlockSpec(memory_space=pl.ANY)
    dma = pltpu.SemaphoreType.DMA
    state = pltpu.VMEM((PAIRS, 2, DH, DH), bf16)
    flops = 2 * rows * d_model * (4 * d_model) + 2 * rows * d_model * (2 * BLK + 4 * DH)
    return pl.pallas_call(
        functools.partial(kernel, n_seq, rows),
        out_shape=jax.ShapeDtypeStruct((rows, d_model), bf16),
        in_specs=[any_spec] * 6,
        out_specs=any_spec,
        scratch_shapes=[
            pltpu.VMEM((rows, d_model), bf16),
            pltpu.VMEM((HALO, d_model), bf16),
            pltpu.VMEM((rows + HALO, d_model), bf16),
            pltpu.VMEM((1, d_model), f32),
            pltpu.VMEM((KW, 3 * d_model), f32),
            pltpu.VMEM((1, d_model), f32),
            pltpu.VMEM((groups, d_model, PW), bf16),
            pltpu.VMEM((PAIRS, d_model, PW), bf16),
            pltpu.VMEM((2, 2, rows + HALO, DH), f32),
            pltpu.VMEM((PAIRS, rows, PW), bf16),
            pltpu.VMEM((PAIRS, rows, PW), bf16),
            pltpu.VMEM((PAIRS, rows, PW), bf16),
            pltpu.VMEM((PAIRS, rows, PW), f32),
            pltpu.VMEM((rows, d_model), bf16),
            pltpu.VMEM((PAIRS, rows, PW), bf16),
            pltpu.VMEM((PAIRS, nblk, 2, DH, DH), f32),
            pltpu.VMEM((nblk, PW, PW), bf16),
            state, state, state, state,
            dma((4,)), dma((groups,)), dma((3,)), dma((PAIRS,)), dma((PAIRS,)),
            dma, dma, dma((PAIRS,)), dma((PAIRS,)), dma((PAIRS,)), dma((PAIRS,)),
        ],
        compiler_params=pltpu.CompilerParams(
            collective_id=0, has_side_effects=True, vmem_limit_bytes=52 * 1024 * 1024
        ),
        cost_estimate=pl.CostEstimate(flops=flops, bytes_accessed=12 << 20, transcendentals=rows * 3 * d_model),
    )(tokens, norm_gain.reshape(1, -1), w_qkv, conv_weight, head_gain.reshape(1, -1), w_out)


def solution(mesh):
    placed = (P(("trace", "seq"), None), P(), P(), P(), P(), P())
    return jax.shard_map(
        functools.partial(local, mesh.shape["seq"]),
        mesh=mesh,
        in_specs=placed,
        out_specs=P(("trace", "seq"), None),
        check_vma=False,
    )
```
